512 devices in a mesh: vol: 64 (over z_lo, y, core), strip: 8 (over z_hi, x).
Axes of the slice: x: 4, y: 8, z: 8 (z_hi: 2, z_lo: 4; z = z_hi * 4 + z_lo), core: 2. Of those that a mesh axis runs over, the one named last changes fastest.
Arguments:
- frames: bfloat16 [128, 1, 2048, 1024], P('vol', None, 'strip'), may hold values from 0.5 to 4
- kappa: float32 [128], P('vol'), may hold values from 0.3 to 3
Outputs:
- dff: bfloat16 [128, 1, 256, 8, 1024], P(None, None, 'vol', 'strip')
- slope: bfloat16 [128, 1, 256, 8, 1024], P(None, None, 'vol', 'strip')
The draws below stay inside these ranges and needn't reach their ends.
All inputs are finite; a program needn't handle non-finite values.
Results may differ from the reference program's by a relative error of at most 0.0097.
Values may be sent and summed in bfloat16 or wider, within the bound.
No kernel may reach another device: no remote copies, remote signals or barrier semaphores. Data moves between devices by JAX's collectives and lax.ppermute only.
A program may use at most 64 MiB of HBM per device.

```python
import math
import jax
import jax.numpy as jnp
from jax import lax

PLANES = 1
NX = 1024
PASSES = 3
BAND = 16
TIMES = 128
SY = 256
NY = 2048
N_STRIP = 8


def level_of(key, shape, shards, low, high):
    def one(dim, blocks):
        draws = jax.random.uniform(jax.random.fold_in(jax.random.fold_in(key, 6), dim), (blocks,), jnp.float32, low / len(shards), high / len(shards))
        return jnp.repeat(jnp.exp(draws), shape[dim] // blocks).reshape((-1,) + (1,) * (len(shape) - dim - 1))

    factor_of = one(*shards[0])
    for cut in shards[1:]:
        factor_of = factor_of * one(*cut)
    return factor_of


def setup_inputs(seed: int = 0) -> dict:
    seeds = jax.random.split(jax.random.key(seed), 3)
    return {
        "frames": jnp.clip(jnp.exp(math.log(4.0) - 2.0794415 * jax.random.uniform(seeds[0], (TIMES, PLANES, NY, NX), jnp.float32) ** level_of(seeds[0], (TIMES, PLANES, NY, NX), ((0, 64), (2, 8)), -0.2, 0.2)), 0.5, 4.0).astype(jnp.bfloat16),
        "kappa": jnp.clip(jnp.exp(math.log(3.0) - 2.3025851 * jax.random.uniform(seeds[1], (TIMES,), jnp.float32) ** level_of(seeds[1], (TIMES,), ((0, 64),), -0.2, 0.2)), 0.3, 3.0),
    }


def flux(diff, kap):
    ratio = diff / kap
    return diff / (1.0 + ratio * ratio)


def advance(extended, kap):
    center = extended[..., 1:-1, :]
    upper = extended[..., :-2, :] - center
    lower = extended[..., 2:, :] - center
    padded = jnp.pad(center, [(0, 0)] * (center.ndim - 1) + [(1, 1)])
    left = padded[..., :-2] - center
    right = padded[..., 2:] - center
    total = flux(upper, kap) + flux(lower, kap) + flux(left, kap) + flux(right, kap)
    return center + 0.2 * total


def smooth_weights(times):
    steps = jnp.arange(times, dtype=jnp.int32)
    gap = jnp.abs(steps[:, None] - steps[None, :])
    raw = jnp.where(gap <= BAND, BAND + 1 - gap, 0).astype(jnp.float32)
    return (raw / jnp.sum(raw, axis=1, keepdims=True)).astype(jnp.bfloat16)


def reference(frames, kappa):
    def one_volume(item):
        volume, kap = item
        field = volume.astype(jnp.float32)
        for step in range(PASSES):
            field = advance(jnp.pad(field, ((0, 0), (1, 1), (0, 0))), kap)
        return field.astype(jnp.bfloat16)

    stored = lax.map(one_volume, (frames, kappa))
    weights = smooth_weights(TIMES)

    def one_plane(plane):
        flat = plane.reshape(TIMES, NY * NX)
        baseline = jnp.dot(weights, flat, preferred_element_type=jnp.float32)
        ratio = (flat.astype(jnp.float32) - baseline) / (baseline + 0.1)
        slope = jnp.concatenate([ratio[1:2] - ratio[0:1], (ratio[2:] - ratio[:-2]) * 0.5, ratio[-1:] - ratio[-2:-1]], axis=0)
        return ratio.reshape(TIMES, NY, NX).astype(jnp.bfloat16), slope.reshape(TIMES, NY, NX).astype(jnp.bfloat16)

    ratio, slope = lax.map(one_plane, jnp.transpose(stored, (1, 0, 2, 3)))

    def layout(field):
        field = jnp.transpose(field, (1, 0, 2, 3)).reshape(TIMES, PLANES, N_STRIP, SY, NX)
        return jnp.transpose(field, (0, 1, 3, 2, 4))

    return layout(ratio), layout(slope)
```

```python
import functools
import math
import numpy as np
import jax
import jax.numpy as jnp
from jax import lax
from jax.experimental import pallas as pl
from jax.experimental.pallas import tpu as pltpu
from jax.sharding import PartitionSpec as P

PASSES = 3
BAND = 16
TIMES = 128
LANES = 128
TILES = 8
ROWS = 256
HALO = 4
STEP = 16
STARTS = (0, 64, 192, 256)
CHUNK = 256
ROOT5 = math.sqrt(5.0)


def band_weights():
    steps = np.arange(TIMES)
    gap = np.abs(steps[:, None] - steps[None, :])
    raw = np.where(gap <= BAND, BAND + 1 - gap, 0).astype(np.float32)
    weights = raw / np.sum(raw, axis=1, keepdims=True, dtype=np.float32)
    spread = np.kron(weights, np.eye(4, dtype=np.float32))
    blocks = [spread[128 * b : 128 * b + 128, k : k + 256] for b, k in enumerate(STARTS)]
    return jnp.asarray(np.concatenate(blocks, axis=0), jnp.bfloat16)


def flux(diff):
    return diff * pl.reciprocal(5.0 + diff * diff, approx=True)


def advance(mid, below, carry):
    shape = mid[0][0].shape
    lane = lax.broadcasted_iota(jnp.int32, shape, 1)
    row = lax.broadcasted_iota(jnp.int32, shape, 0)
    last, first, top = lane == LANES - 1, lane == 0, row == 0
    carry = list(carry)
    new = []
    for k, pieces in enumerate(mid):
        line = []
        turned = pltpu.roll(pieces[0], LANES - 1, 1)
        before = flux(pieces[0])
        for i, value in enumerate(pieces):
            later = pltpu.roll(pieces[i + 1], LANES - 1, 1) if i + 1 < len(pieces) else jnp.zeros_like(value)
            right = flux(jnp.where(last, later, turned) - value)
            turned = later
            moved = pltpu.roll(right, 1, 1)
            left = jnp.where(first, before, moved)
            before = moved
            down = flux(below[k][i] - value)
            sunk = pltpu.roll(down, 1, 0)
            up = jnp.where(top, carry[i], sunk)
            carry[i] = sunk
            line.append(value + ((down - up) + (right - left)))
        new.append(line)
    return new, carry


def inner_kernel(kappa_ref, frames_ref, out_ref, field):
    for v in range(2):
        unit = ROOT5 / jnp.full((STEP, LANES), kappa_ref[v], jnp.float32)

        def load(j, _, v=v, unit=unit):
            at = pl.multiple_of(j * STEP, STEP)
            for i in range(TILES):
                value = frames_ref[v, pl.ds(at, STEP), i * LANES : (i + 1) * LANES]
                field[v, i, pl.ds(at, STEP), :] = value.astype(jnp.float32) * unit
            return 0

        lax.fori_loop(0, ROWS // STEP, load, 0)
        for i in range(TILES):
            field[v, i, ROWS : ROWS + 8, :] = jnp.zeros((8, LANES), jnp.float32)

    zero = jnp.zeros((8, LANES), jnp.float32)

    def read(v, at):
        mid = [[field[v, i, pl.ds(at + 8 * k, 8), :] for i in range(TILES)] for k in range(STEP // 8)]
        below = [[field[v, i, pl.ds(at + 8 * k + 1, 8), :] for i in range(TILES)] for k in range(STEP // 8)]
        return mid, below

    for p in range(PASSES - 1):

        def step(j, carry):
            at = pl.multiple_of(j * STEP, STEP)
            later = []
            for v in range(2):
                mid, below = read(v, at)
                new, after = advance(mid, below, carry[v])
                for k in range(STEP // 8):
                    for i in range(TILES):
                        field[v, i, pl.ds(at + 8 * k, 8), :] = new[k][i]
                later.append(after)
            return later

        lax.fori_loop(0, ROWS // STEP, step, [[zero] * TILES] * 2)

    units = [jnp.full((8, LANES), kappa_ref[v], jnp.float32) * (1.0 / ROOT5) for v in range(2)]
    low = lax.broadcasted_iota(jnp.int32, (8, LANES), 0) < 4

    def step(j, carry):
        at = pl.multiple_of(j * STEP, STEP)
        later, both = [], []
        for v in range(2):
            mid, below = read(v, at)
            new, after = advance(mid, below, carry[v])
            later.append(after)
            both.append(new)
        for k in range(STEP // 8):
            for i in range(TILES):
                a, b = both[0][k][i] * units[0], both[1][k][i] * units[1]
                even = jnp.where(low, a, pltpu.roll(b, 4, 0))
                odd = jnp.where(low, pltpu.roll(a, 4, 0), b)
                spot = j * (STEP // 8) + k
                out_ref[spot, 0, :, i * LANES : (i + 1) * LANES] = even.astype(jnp.bfloat16)
                out_ref[spot, 1, :, i * LANES : (i + 1) * LANES] = odd.astype(jnp.bfloat16)
        return later

    lax.fori_loop(0, ROWS // STEP, step, [[zero] * TILES] * 2)


def edge_kernel(kappa_ref, head_ref, tail_ref, above_ref, under_ref, _, out_ref, sems, field, blocks):
    strip = lax.axis_index("strip")
    inside = (
        jnp.where(strip == 0, 0.0, 1.0).astype(jnp.float32),
        jnp.where(strip == lax.axis_size("strip") - 1, 0.0, 1.0).astype(jnp.float32),
    )
    low = lax.broadcasted_iota(jnp.int32, (8, LANES), 0) < 4
    zero = jnp.zeros((8, LANES), jnp.float32)
    spots = [slice(i * LANES, (i + 1) * LANES) for i in range(TILES)]
    done = []
    for v in range(2):
        unit = ROOT5 / jnp.full((1, LANES), kappa_ref[v], jnp.float32)
        sides = []
        for side in range(2):
            if side == 0:
                own = head_ref[v].astype(jnp.float32)[0:8]
                far = above_ref[v].astype(jnp.float32)
                window = [jnp.concatenate([far, far], axis=0), own]
            else:
                own = tail_ref[v].astype(jnp.float32)[8:16]
                far = under_ref[v].astype(jnp.float32)
                window = [own, jnp.concatenate([far, far], axis=0)]
            mid = [[w[:, s] * unit for s in spots] for w in window]
            for p in range(PASSES):
                for k in range(2):
                    for i in range(TILES):
                        field[2 * v + side, i, 8 * k : 8 * k + 8, :] = mid[k][i]
                below = [[field[2 * v + side, i, 8 * k + 1 : 8 * k + 9, :] for i in range(TILES)] for k in range(2)]
                mid, _unused = advance(mid, below, [zero] * TILES)
                mid[side] = [value * inside[side] for value in mid[side]]
            sides.append([value * (kappa_ref[v] * (1.0 / ROOT5)) for value in mid[1 - side]])
        done.append(sides)
    for i in range(TILES):
        top = jnp.where(low, done[0][0][i], pltpu.roll(done[1][0][i], 4, 0))
        end = jnp.where(low, pltpu.roll(done[0][1][i], 4, 0), done[1][1][i])
        blocks[0, :, spots[i]] = top.astype(jnp.bfloat16)
        blocks[1, :, spots[i]] = end.astype(jnp.bfloat16)
    copies = [
        pltpu.make_async_copy(blocks.at[0], out_ref.at[0, 0], sems.at[0]),
        pltpu.make_async_copy(blocks.at[1], out_ref.at[31, 1], sems.at[1]),
    ]
    for copy in copies:
        copy.start()
    for copy in copies:
        copy.wait()


def detrend_kernel(weights_ref, stored_ref, dff_ref, slope_ref, ratio):
    stored = stored_ref[...].reshape(4 * TIMES, CHUNK)
    for b, k in enumerate(STARTS):
        baseline = jnp.dot(
            weights_ref[128 * b : 128 * b + 128, :], stored[k : k + 256], preferred_element_type=jnp.float32
        )
        value = stored[128 * b : 128 * b + 128].astype(jnp.float32)
        ratio[16 * b : 16 * b + 16] = ((value - baseline) / (baseline + 0.1)).reshape(16, 8, CHUNK)

    low = lax.broadcasted_iota(jnp.int32, (8, LANES), 0) < 4
    for i in range(CHUNK // LANES):
        spot = slice(i * LANES, (i + 1) * LANES)
        own = ratio[0, :, spot]
        turned = pltpu.roll(own, 4, 0)
        previous = None
        for j in range(TIMES // 2):
            if j + 1 < TIMES // 2:
                other = ratio[j + 1, :, spot]
                other_turned = pltpu.roll(other, 4, 0)
                between = jnp.where(low, turned, other_turned)
            else:
                other = other_turned = None
                between = turned
            if previous is None:
                slope = jnp.where(low, between - own, 0.5 * (between - turned))
            elif other is None:
                slope = jnp.where(low, 0.5 * (between - previous), own - previous)
            else:
                slope = 0.5 * (between - previous)
            dff_ref[j, 0, :, spot] = own[0:4].astype(jnp.bfloat16)
            dff_ref[j, 1, :, spot] = turned[0:4].astype(jnp.bfloat16)
            slope_ref[j, 0, :, spot] = slope[0:4].astype(jnp.bfloat16)
            slope_ref[j, 1, :, spot] = pltpu.roll(slope, 4, 0)[0:4].astype(jnp.bfloat16)
            own, turned, previous = other, other_turned, between


VMEM = pl.BlockSpec(memory_space=pltpu.VMEM)
SMEM = pl.BlockSpec(memory_space=pltpu.SMEM)
ANY = pl.BlockSpec(memory_space=pl.ANY)


def diffuse(frames, kappa):
    devices = lax.axis_size("strip")
    up = [(i, i + 1) for i in range(devices - 1)]
    down = [(i + 1, i) for i in range(devices - 1)]
    above = lax.ppermute(frames[:, ROWS - HALO :], "strip", up)
    under = lax.ppermute(frames[:, :HALO], "strip", down)
    params = pltpu.CompilerParams(vmem_limit_bytes=24 * 1024 * 1024)
    inner = pl.pallas_call(
        inner_kernel,
        out_shape=jax.ShapeDtypeStruct((32, 2, 8, 1024), jnp.bfloat16),
        in_specs=[SMEM, VMEM],
        out_specs=VMEM,
        scratch_shapes=[pltpu.VMEM((2, TILES, ROWS + 8, LANES), jnp.float32)],
        compiler_params=params,
        cost_estimate=pl.CostEstimate(flops=60_000_000, bytes_accessed=2 << 20, transcendentals=3 << 20),
        name="inner",
    )(kappa, frames)
    whole = pl.pallas_call(
        edge_kernel,
        grid=(1,),
        out_shape=jax.ShapeDtypeStruct((32, 2, 8, 1024), jnp.bfloat16),
        in_specs=[
            SMEM,
            pl.BlockSpec((2, 16, 1024), lambda i: (0, 0, 0)),
            pl.BlockSpec((2, 16, 1024), lambda i: (0, 15, 0)),
            pl.BlockSpec((2, HALO, 1024), lambda i: (0, 0, 0)),
            pl.BlockSpec((2, HALO, 1024), lambda i: (0, 0, 0)),
            ANY,
        ],
        out_specs=ANY,
        scratch_shapes=[
            pltpu.SemaphoreType.DMA((2,)),
            pltpu.VMEM((4, TILES, 24, LANES), jnp.float32),
            pltpu.VMEM((2, 8, 1024), jnp.bfloat16),
        ],
        input_output_aliases={5: 0},
        compiler_params=params,
        name="edges",
    )(kappa, frames, frames, above, under, inner)
    return whole.reshape(64, 8, 1024)


def detrend(stored):
    block = pl.BlockSpec((64, 2, 4, CHUNK), lambda i: (0, 0, 0, i))
    shape = jax.ShapeDtypeStruct((64, 2, 4, 1024), jnp.bfloat16)
    return pl.pallas_call(
        detrend_kernel,
        grid=(1024 // CHUNK,),
        out_shape=[shape, shape],
        in_specs=[pl.BlockSpec((512, 256), lambda i: (0, 0)), pl.BlockSpec((64, 8, CHUNK), lambda i: (0, 0, i))],
        out_specs=[block, block],
        scratch_shapes=[pltpu.VMEM((64, 8, CHUNK), jnp.float32)],
        compiler_params=pltpu.CompilerParams(vmem_limit_bytes=24 * 1024 * 1024),
        name="detrend",
    )(band_weights(), stored)


def local(frames, kappa):
    blocks = diffuse(frames.reshape(2, ROWS, 1024), kappa)
    stored = lax.all_to_all(blocks, "vol", split_axis=0, concat_axis=0, tiled=True)
    dff, slope = detrend(stored)
    return dff.reshape(128, 1, 4, 1, 1024), slope.reshape(128, 1, 4, 1, 1024)


def solution(mesh):
    out = P(None, None, "vol", "strip", None)
    return jax.shard_map(
        local,
        mesh=mesh,
        in_specs=(P("vol", None, "strip", None), P("vol")),
        out_specs=(out, out),
        check_vma=False,
    )
```

```python
import functools
import math
import numpy as np
import jax
import jax.numpy as jnp
from jax import lax
from jax.experimental import pallas as pl
from jax.experimental.pallas import tpu as pltpu
from jax.sharding import PartitionSpec as P

PASSES = 3
BAND = 16
TIMES = 128
LANES = 128
TILES = 8
ROWS = 256
HALO = 4
GROUP = 4
WIDE = GROUP * LANES
MIX = 64
STARTS = (0, 64, 192, 256)
CHUNK = 512
ROOT5 = math.sqrt(5.0)


def band_weights():
    steps = np.arange(TIMES)
    gap = np.abs(steps[:, None] - steps[None, :])
    raw = np.where(gap <= BAND, BAND + 1 - gap, 0).astype(np.float32)
    weights = raw / np.sum(raw, axis=1, keepdims=True, dtype=np.float32)
    spread = np.kron(weights, np.eye(4, dtype=np.float32))
    blocks = [spread[128 * b : 128 * b + 128, k : k + 256] for b, k in enumerate(STARTS)]
    return jnp.asarray(np.concatenate(blocks, axis=0), jnp.bfloat16)


def flux(diff):
    return diff * pl.reciprocal(5.0 + diff * diff, approx=True)


def advance(pieces, below, above_flow, group):
    shape = pieces[0].shape
    lane = lax.broadcasted_iota(jnp.int32, shape, 1)
    last, first = lane == LANES - 1, lane == 0
    new = []
    before = flux(pieces[0])
    turned = pltpu.roll(pieces[0], LANES - 1, 1)
    for g in range(0, TILES, group):
        later = pltpu.roll(pieces[g + group], LANES - 1, 1) if g + group < TILES else jnp.zeros(shape, jnp.float32)
        right = list(pieces[g + 1 : g + group]) + [jnp.where(last, later, turned)]
        turned = later
        flow = [flux(right[t] - pieces[g + t]) for t in range(group)]
        moved = pltpu.roll(flow[-1], 1, 1)
        left = [jnp.where(first, before, moved)] + flow[:-1]
        before = moved
        for t in range(group):
            i = g + t
            down = flux(below[i] - pieces[i])
            up = above_flow(i, down)
            new.append(pieces[i] + ((down - up) + (flow[t] - left[t])))
    return new


def inner_kernel(kappa_ref, frames_ref, out_ref, ends_ref, field, flows, spread, gather, packed):
    source = lax.broadcasted_iota(jnp.int32, (WIDE, LANES), 0)
    lane = lax.broadcasted_iota(jnp.int32, (WIDE, LANES), 1)
    for t in range(GROUP):
        spread[:, t * LANES : (t + 1) * LANES] = (source == lane * GROUP + t).astype(jnp.float32).astype(jnp.bfloat16)
        place = (source & (LANES - 1)) * GROUP + lax.shift_right_logical(source, 7)
        gather[:, t * LANES : (t + 1) * LANES] = (place == lane + t * LANES).astype(jnp.float32).astype(jnp.bfloat16)
    units = [ROOT5 / jnp.full((8, LANES), kappa_ref[v], jnp.float32) for v in range(2)]
    backs = [jnp.full((8, LANES), kappa_ref[v], jnp.float32) * (1.0 / ROOT5) for v in range(2)]
    low = lax.broadcasted_iota(jnp.int32, (8, LANES), 0) < 4
    zero = jnp.zeros((8, LANES), jnp.float32)
    groups = TILES // GROUP
    for v in range(2):
        for i in range(TILES):
            field[v, i, ROWS : ROWS + 8, :] = zero
            flows[v, i, 0:8, :] = zero

    def fill(at):
        rows = [frames_ref[v, at : at + MIX, g * WIDE : (g + 1) * WIDE] for v in range(2) for g in range(groups)]
        value = jnp.dot(jnp.concatenate(rows, axis=0), spread[...], preferred_element_type=jnp.float32)
        for v in range(2):
            for i in range(TILES):
                g, t = i // GROUP, i % GROUP
                start = (v * groups + g) * MIX
                field[v, i, at : at + MIX, :] = value[start : start + MIX, t * LANES : (t + 1) * LANES] * units[v][0:1]

    def move(v, at):
        def above_flow(i, down):
            flows[v, i, pl.ds(at + 8, 8), :] = down
            return flows[v, i, pl.ds(at + 7, 8), :]

        pieces = [field[v, i, pl.ds(at, 8), :] for i in range(TILES)]
        below = [field[v, i, pl.ds(at + 1, 8), :] for i in range(TILES)]
        return advance(pieces, below, above_flow, GROUP)

    def empty(at):
        rows = [packed[at : at + 2 * MIX, g * WIDE : (g + 1) * WIDE] for g in range(groups)]
        value = jnp.dot(jnp.concatenate(rows, axis=0), gather[...], preferred_element_type=jnp.float32)
        value = value.astype(jnp.bfloat16)
        for g in range(groups):
            out_ref[at // 8 : (at + 2 * MIX) // 8, :, g * WIDE : (g + 1) * WIDE] = value[
                g * 2 * MIX : (g + 1) * 2 * MIX
            ].reshape(2 * MIX // 8, 8, WIDE)

    fill(0)
    for p in range(PASSES):
        for start in range(0, ROWS, MIX):
            if p == 0 and start + MIX < ROWS:
                fill(start + MIX)
            if p == PASSES - 1 and start:
                empty(2 * (start - MIX))
            for at in range(start, start + MIX, 8):
                new = [move(v, at) for v in range(2)]
                for i in range(TILES):
                    if p < PASSES - 1:
                        field[0, i, at : at + 8, :] = new[0][i]
                        field[1, i, at : at + 8, :] = new[1][i]
                    else:
                        a, b = new[0][i] * backs[0], new[1][i] * backs[1]
                        even = jnp.where(low, a, pltpu.roll(b, 4, 0))
                        odd = jnp.where(low, pltpu.roll(a, 4, 0), b)
                        both = jnp.concatenate([even, odd], axis=0).astype(jnp.bfloat16)
                        packed[2 * at : 2 * at + 16, i * LANES : (i + 1) * LANES] = both
    empty(2 * (ROWS - MIX))
    ends_ref[:, :16] = frames_ref[:, :16]
    ends_ref[:, 16:] = frames_ref[:, ROWS - 16 :]


def edge_kernel(kappa_ref, ends_ref, above_ref, under_ref, _, out_ref, sems, field, flows, blocks):
    strip = lax.axis_index("strip")
    inside = (
        jnp.where(strip == 0, 0.0, 1.0).astype(jnp.float32),
        jnp.where(strip == lax.axis_size("strip") - 1, 0.0, 1.0).astype(jnp.float32),
    )
    low = lax.broadcasted_iota(jnp.int32, (8, LANES), 0) < 4
    zero = jnp.zeros((8, LANES), jnp.float32)
    spots = [slice(i * LANES, (i + 1) * LANES) for i in range(TILES)]
    for n in range(4):
        for i in range(TILES):
            field[n, i, 16:24, :] = zero
            flows[n, i, 0:8, :] = zero
    done = []
    for v in range(2):
        unit = ROOT5 / jnp.full((1, LANES), kappa_ref[v], jnp.float32)
        sides = []
        for side in range(2):
            if side == 0:
                own = ends_ref[v, :16].astype(jnp.float32)[0:8]
                far = above_ref[v].astype(jnp.float32)
                window = [jnp.concatenate([far, far], axis=0), own]
            else:
                own = ends_ref[v, 16:].astype(jnp.float32)[8:16]
                far = under_ref[v].astype(jnp.float32)
                window = [own, jnp.concatenate([far, far], axis=0)]
            mid = [[w[:, s] * unit for s in spots] for w in window]
            for p in range(PASSES):
                for k in range(2):
                    for i in range(TILES):
                        field[2 * v + side, i, 8 * k : 8 * k + 8, :] = mid[k][i]
                for k in range(2):
                    below = [field[2 * v + side, i, 8 * k + 1 : 8 * k + 9, :] for i in range(TILES)]

                    def above_flow(i, down, at=8 * k, n=2 * v + side):
                        flows[n, i, at + 8 : at + 16, :] = down
                        return flows[n, i, at + 7 : at + 15, :]

                    mid[k] = advance(mid[k], below, above_flow, 1)
                mid[side] = [value * inside[side] for value in mid[side]]
            sides.append([value * (kappa_ref[v] * (1.0 / ROOT5)) for value in mid[1 - side]])
        done.append(sides)
    for i in range(TILES):
        top = jnp.where(low, done[0][0][i], pltpu.roll(done[1][0][i], 4, 0))
        end = jnp.where(low, pltpu.roll(done[0][1][i], 4, 0), done[1][1][i])
        blocks[0, :, spots[i]] = top.astype(jnp.bfloat16)
        blocks[1, :, spots[i]] = end.astype(jnp.bfloat16)
    copies = [
        pltpu.make_async_copy(blocks.at[0], out_ref.at[0], sems.at[0]),
        pltpu.make_async_copy(blocks.at[1], out_ref.at[63], sems.at[1]),
    ]
    for copy in copies:
        copy.start()
    for copy in copies:
        copy.wait()


def detrend_kernel(weights_ref, stored_ref, dff_ref, slope_ref, ratio):
    stored = stored_ref[...].reshape(4 * TIMES, CHUNK)
    for b, k in enumerate(STARTS):
        baseline = jnp.dot(
            weights_ref[128 * b : 128 * b + 128, :], stored[k : k + 256], preferred_element_type=jnp.float32
        )
        value = stored[128 * b : 128 * b + 128].astype(jnp.float32)
        ratio[16 * b : 16 * b + 16] = ((value - baseline) / (baseline + 0.1)).reshape(16, 8, CHUNK)

    low = lax.broadcasted_iota(jnp.int32, (8, LANES), 0) < 4
    for i in range(CHUNK // LANES):
        spot = slice(i * LANES, (i + 1) * LANES)
        own = ratio[0, :, spot]
        turned = pltpu.roll(own, 4, 0)
        previous = None
        for j in range(TIMES // 2):
            if j + 1 < TIMES // 2:
                other = ratio[j + 1, :, spot]
                other_turned = pltpu.roll(other, 4, 0)
                between = jnp.where(low, turned, other_turned)
            else:
                other = other_turned = None
                between = turned
            if previous is None:
                slope = jnp.where(low, between - own, 0.5 * (between - turned))
            elif other is None:
                slope = jnp.where(low, 0.5 * (between - previous), own - previous)
            else:
                slope = 0.5 * (between - previous)
            dff_ref[j, 0, :, spot] = own[0:4].astype(jnp.bfloat16)
            dff_ref[j, 1, :, spot] = turned[0:4].astype(jnp.bfloat16)
            slope_ref[j, 0, :, spot] = slope[0:4].astype(jnp.bfloat16)
            slope_ref[j, 1, :, spot] = pltpu.roll(slope, 4, 0)[0:4].astype(jnp.bfloat16)
            own, turned, previous = other, other_turned, between


VMEM = pl.BlockSpec(memory_space=pltpu.VMEM)
SMEM = pl.BlockSpec(memory_space=pltpu.SMEM)
ANY = pl.BlockSpec(memory_space=pl.ANY)


def diffuse(frames, kappa):
    devices = lax.axis_size("strip")
    up = [(i, i + 1) for i in range(devices - 1)]
    down = [(i + 1, i) for i in range(devices - 1)]
    above = lax.ppermute(frames[:, ROWS - HALO :], "strip", up)
    under = lax.ppermute(frames[:, :HALO], "strip", down)
    params = pltpu.CompilerParams(vmem_limit_bytes=24 * 1024 * 1024)
    inner, ends = pl.pallas_call(
        inner_kernel,
        out_shape=[
            jax.ShapeDtypeStruct((64, 8, 1024), jnp.bfloat16),
            jax.ShapeDtypeStruct((2, 32, 1024), jnp.bfloat16),
        ],
        in_specs=[SMEM, VMEM],
        out_specs=[VMEM, VMEM],
        scratch_shapes=[
            pltpu.VMEM((2, TILES, ROWS + 8, LANES), jnp.float32),
            pltpu.VMEM((2, TILES, ROWS + 8, LANES), jnp.float32),
            pltpu.VMEM((WIDE, WIDE), jnp.bfloat16),
            pltpu.VMEM((WIDE, WIDE), jnp.bfloat16),
            pltpu.VMEM((2 * ROWS, 1024), jnp.bfloat16),
        ],
        compiler_params=params,
        cost_estimate=pl.CostEstimate(flops=60_000_000, bytes_accessed=2 << 20, transcendentals=3 << 20),
        name="inner",
    )(kappa, frames)
    whole = pl.pallas_call(
        edge_kernel,
        out_shape=jax.ShapeDtypeStruct((64, 8, 1024), jnp.bfloat16),
        in_specs=[SMEM, VMEM, VMEM, VMEM, ANY],
        out_specs=ANY,
        scratch_shapes=[
            pltpu.SemaphoreType.DMA((2,)),
            pltpu.VMEM((4, TILES, 24, LANES), jnp.float32),
            pltpu.VMEM((4, TILES, 24, LANES), jnp.float32),
            pltpu.VMEM((2, 8, 1024), jnp.bfloat16),
        ],
        input_output_aliases={4: 0},
        compiler_params=params,
        name="edges",
    )(kappa, ends, above, under, inner)
    return whole


def detrend(stored):
    block = pl.BlockSpec((64, 2, 4, CHUNK), lambda i: (0, 0, 0, i))
    shape = jax.ShapeDtypeStruct((64, 2, 4, 1024), jnp.bfloat16)
    return pl.pallas_call(
        detrend_kernel,
        grid=(1024 // CHUNK,),
        out_shape=[shape, shape],
        in_specs=[pl.BlockSpec((512, 256), lambda i: (0, 0)), pl.BlockSpec((64, 8, CHUNK), lambda i: (0, 0, i))],
        out_specs=[block, block],
        scratch_shapes=[pltpu.VMEM((64, 8, CHUNK), jnp.float32)],
        compiler_params=pltpu.CompilerParams(vmem_limit_bytes=24 * 1024 * 1024),
        name="detrend",
    )(band_weights(), stored)


def local(frames, kappa):
    blocks = diffuse(frames.reshape(2, ROWS, 1024), kappa)
    stored = lax.all_to_all(blocks, "vol", split_axis=0, concat_axis=0, tiled=True)
    dff, slope = detrend(stored)
    return dff.reshape(128, 1, 4, 1, 1024), slope.reshape(128, 1, 4, 1, 1024)


def solution(mesh):
    out = P(None, None, "vol", "strip", None)
    return jax.shard_map(
        local,
        mesh=mesh,
        in_specs=(P("vol", None, "strip", None), P("vol")),
        out_specs=(out, out),
        check_vma=False,
    )
```

```python
import functools
import math
import numpy as np
import jax
import jax.numpy as jnp
from jax import lax
from jax.experimental import pallas as pl
from jax.experimental.pallas import tpu as pltpu
from jax.sharding import PartitionSpec as P

PASSES = 3
BAND = 16
TIMES = 128
LANES = 128
TILES = 8
ROWS = 256
HALO = 4
GROUP = 4
WIDE = GROUP * LANES
MIX = 64
STARTS = (0, 64, 192, 256)
CHUNK = 512
ROOT5 = math.sqrt(5.0)


def band_weights():
    steps = np.arange(TIMES)
    gap = np.abs(steps[:, None] - steps[None, :])
    raw = np.where(gap <= BAND, BAND + 1 - gap, 0).astype(np.float32)
    weights = raw / np.sum(raw, axis=1, keepdims=True, dtype=np.float32)
    spread = np.kron(weights, np.eye(4, dtype=np.float32))
    blocks = [spread[128 * b : 128 * b + 128, k : k + 256] for b, k in enumerate(STARTS)]
    return jnp.asarray(np.concatenate(blocks, axis=0), jnp.bfloat16)


def flux(diff):
    return diff * pl.reciprocal(5.0 + diff * diff, approx=True)


def advance(pieces, below, above_flow, group):
    shape = pieces[0].shape
    lane = lax.broadcasted_iota(jnp.int32, shape, 1)
    last, first = lane == LANES - 1, lane == 0
    new = []
    before = flux(pieces[0])
    turned = pltpu.roll(pieces[0], LANES - 1, 1)
    for g in range(0, TILES, group):
        later = pltpu.roll(pieces[g + group], LANES - 1, 1) if g + group < TILES else jnp.zeros(shape, jnp.float32)
        right = list(pieces[g + 1 : g + group]) + [jnp.where(last, later, turned)]
        turned = later
        flow = [flux(right[t] - pieces[g + t]) for t in range(group)]
        moved = pltpu.roll(flow[-1], 1, 1)
        left = [jnp.where(first, before, moved)] + flow[:-1]
        before = moved
        for t in range(group):
            i = g + t
            down = flux(below[i] - pieces[i])
            up = above_flow(i, down)
            new.append(pieces[i] + ((down - up) + (flow[t] - left[t])))
    return new


def inner_kernel(kappa_ref, frames_ref, out_ref, ends_ref, field, flows, spread, gather, packed):
    source = lax.broadcasted_iota(jnp.int32, (WIDE, LANES), 0)
    lane = lax.broadcasted_iota(jnp.int32, (WIDE, LANES), 1)
    for t in range(GROUP):
        spread[:, t * LANES : (t + 1) * LANES] = (source == lane * GROUP + t).astype(jnp.float32).astype(jnp.bfloat16)
        place = (source & (LANES - 1)) * GROUP + lax.shift_right_logical(source, 7)
        gather[:, t * LANES : (t + 1) * LANES] = (place == lane + t * LANES).astype(jnp.float32).astype(jnp.bfloat16)
    units = [ROOT5 / jnp.full((8, LANES), kappa_ref[v], jnp.float32) for v in range(2)]
    backs = [jnp.full((8, LANES), kappa_ref[v], jnp.float32) * (1.0 / ROOT5) for v in range(2)]
    low = lax.broadcasted_iota(jnp.int32, (8, LANES), 0) < 4
    zero = jnp.zeros((8, LANES), jnp.float32)
    groups = TILES // GROUP
    for v in range(2):
        for i in range(TILES):
            field[v, i, ROWS : ROWS + 8, :] = zero
            flows[v, i, 0:8, :] = zero

    def fill(at):
        rows = [frames_ref[v, at : at + MIX, g * WIDE : (g + 1) * WIDE] for v in range(2) for g in range(groups)]
        value = jnp.dot(jnp.concatenate(rows, axis=0), spread[...], preferred_element_type=jnp.float32)
        for v in range(2):
            for i in range(TILES):
                g, t = i // GROUP, i % GROUP
                start = (v * groups + g) * MIX
                field[v, i, at : at + MIX, :] = value[start : start + MIX, t * LANES : (t + 1) * LANES] * units[v][0:1]

    def move(v, at):
        def above_flow(i, down):
            flows[v, i, pl.ds(at + 8, 8), :] = down
            return flows[v, i, pl.ds(at + 7, 8), :]

        pieces = [field[v, i, pl.ds(at, 8), :] for i in range(TILES)]
        below = [field[v, i, pl.ds(at + 1, 8), :] for i in range(TILES)]
        return advance(pieces, below, above_flow, GROUP)

    def empty(at):
        rows = [packed[at : at + 2 * MIX, g * WIDE : (g + 1) * WIDE] for g in range(groups)]
        value = jnp.dot(jnp.concatenate(rows, axis=0), gather[...], preferred_element_type=jnp.float32)
        value = value.astype(jnp.bfloat16)
        for g in range(groups):
            out_ref[at // 8 : (at + 2 * MIX) // 8, :, g * WIDE : (g + 1) * WIDE] = value[
                g * 2 * MIX : (g + 1) * 2 * MIX
            ].reshape(2 * MIX // 8, 8, WIDE)

    fill(0)
    for p in range(PASSES):
        for start in range(0, ROWS, MIX):
            if p == 0 and start + MIX < ROWS:
                fill(start + MIX)
            if p == PASSES - 1 and start:
                empty(2 * (start - MIX))
            for at in range(start, start + MIX, 8):
                new = [move(v, at) for v in range(2)]
                for i in range(TILES):
                    if p < PASSES - 1:
                        field[0, i, at : at + 8, :] = new[0][i]
                        field[1, i, at : at + 8, :] = new[1][i]
                    else:
                        a, b = new[0][i] * backs[0], new[1][i] * backs[1]
                        even = jnp.where(low, a, pltpu.roll(b, 4, 0))
                        odd = jnp.where(low, pltpu.roll(a, 4, 0), b)
                        both = jnp.concatenate([even, odd], axis=0).astype(jnp.bfloat16)
                        packed[2 * at : 2 * at + 16, i * LANES : (i + 1) * LANES] = both
    empty(2 * (ROWS - MIX))
    ends_ref[:, :16] = frames_ref[:, :16]
    ends_ref[:, 16:] = frames_ref[:, ROWS - 16 :]


def edge_kernel(kappa_ref, ends_ref, one_ref, two_ref, _, out_ref, sems, field, flows, blocks):
    strip = lax.axis_index("strip")
    even = lax.rem(strip, 2) == 0
    inside = (
        jnp.where(strip == 0, 0.0, 1.0).astype(jnp.float32),
        jnp.where(strip == lax.axis_size("strip") - 1, 0.0, 1.0).astype(jnp.float32),
    )
    low = lax.broadcasted_iota(jnp.int32, (8, LANES), 0) < 4
    zero = jnp.zeros((8, LANES), jnp.float32)
    spots = [slice(i * LANES, (i + 1) * LANES) for i in range(TILES)]
    for n in range(4):
        for i in range(TILES):
            field[n, i, 16:24, :] = zero
            flows[n, i, 0:8, :] = zero
    done = []
    for v in range(2):
        unit = ROOT5 / jnp.full((1, LANES), kappa_ref[v], jnp.float32)
        sides = []
        for side in range(2):
            if side == 0:
                own = ends_ref[v, :16].astype(jnp.float32)[0:8]
                far = jnp.where(even, two_ref[v].astype(jnp.float32), one_ref[v].astype(jnp.float32))
                window = [jnp.concatenate([far, far], axis=0), own]
            else:
                own = ends_ref[v, 16:].astype(jnp.float32)[8:16]
                far = jnp.where(even, one_ref[v].astype(jnp.float32), two_ref[v].astype(jnp.float32))
                window = [own, jnp.concatenate([far, far], axis=0)]
            mid = [[w[:, s] * unit for s in spots] for w in window]
            for p in range(PASSES):
                for k in range(2):
                    for i in range(TILES):
                        field[2 * v + side, i, 8 * k : 8 * k + 8, :] = mid[k][i]
                for k in range(2):
                    below = [field[2 * v + side, i, 8 * k + 1 : 8 * k + 9, :] for i in range(TILES)]

                    def above_flow(i, down, at=8 * k, n=2 * v + side):
                        flows[n, i, at + 8 : at + 16, :] = down
                        return flows[n, i, at + 7 : at + 15, :]

                    mid[k] = advance(mid[k], below, above_flow, 1)
                mid[side] = [value * inside[side] for value in mid[side]]
            sides.append([value * (kappa_ref[v] * (1.0 / ROOT5)) for value in mid[1 - side]])
        done.append(sides)
    for i in range(TILES):
        top = jnp.where(low, done[0][0][i], pltpu.roll(done[1][0][i], 4, 0))
        end = jnp.where(low, pltpu.roll(done[0][1][i], 4, 0), done[1][1][i])
        blocks[0, :, spots[i]] = top.astype(jnp.bfloat16)
        blocks[1, :, spots[i]] = end.astype(jnp.bfloat16)
    copies = [
        pltpu.make_async_copy(blocks.at[0], out_ref.at[0], sems.at[0]),
        pltpu.make_async_copy(blocks.at[1], out_ref.at[63], sems.at[1]),
    ]
    for copy in copies:
        copy.start()
    for copy in copies:
        copy.wait()


def detrend_kernel(weights_ref, stored_ref, dff_ref, slope_ref, ratio):
    stored = stored_ref[...].reshape(4 * TIMES, CHUNK)
    for b, k in enumerate(STARTS):
        baseline = jnp.dot(
            weights_ref[128 * b : 128 * b + 128, :], stored[k : k + 256], preferred_element_type=jnp.float32
        )
        value = stored[128 * b : 128 * b + 128].astype(jnp.float32)
        ratio[16 * b : 16 * b + 16] = ((value - baseline) / (baseline + 0.1)).reshape(16, 8, CHUNK)

    low = lax.broadcasted_iota(jnp.int32, (8, LANES), 0) < 4
    for i in range(CHUNK // LANES):
        spot = slice(i * LANES, (i + 1) * LANES)
        own = ratio[0, :, spot]
        turned = pltpu.roll(own, 4, 0)
        previous = None
        for j in range(TIMES // 2):
            if j + 1 < TIMES // 2:
                other = ratio[j + 1, :, spot]
                other_turned = pltpu.roll(other, 4, 0)
                between = jnp.where(low, turned, other_turned)
            else:
                other = other_turned = None
                between = turned
            if previous is None:
                slope = jnp.where(low, between - own, 0.5 * (between - turned))
            elif other is None:
                slope = jnp.where(low, 0.5 * (between - previous), own - previous)
            else:
                slope = 0.5 * (between - previous)
            dff_ref[j, 0, :, spot] = own[0:4].astype(jnp.bfloat16)
            dff_ref[j, 1, :, spot] = turned[0:4].astype(jnp.bfloat16)
            slope_ref[j, 0, :, spot] = slope[0:4].astype(jnp.bfloat16)
            slope_ref[j, 1, :, spot] = pltpu.roll(slope, 4, 0)[0:4].astype(jnp.bfloat16)
            own, turned, previous = other, other_turned, between


VMEM = pl.BlockSpec(memory_space=pltpu.VMEM)
SMEM = pl.BlockSpec(memory_space=pltpu.SMEM)
ANY = pl.BlockSpec(memory_space=pl.ANY)


def diffuse(frames, kappa):
    devices = lax.axis_size("strip")
    even = lax.rem(lax.axis_index("strip"), 2) == 0
    top, bottom = frames[:, :HALO], frames[:, ROWS - HALO :]
    first = [pair for i in range(0, devices - 1, 2) for pair in ((i, i + 1), (i + 1, i))]
    second = [pair for i in range(1, devices - 1, 2) for pair in ((i, i + 1), (i + 1, i))]
    one, two = lax.optimization_barrier((jnp.where(even, bottom, top), jnp.where(even, top, bottom)))
    one = lax.ppermute(one, "strip", first)
    two = lax.ppermute(two, "strip", second)
    params = pltpu.CompilerParams(vmem_limit_bytes=24 * 1024 * 1024)
    inner, ends = pl.pallas_call(
        inner_kernel,
        out_shape=[
            jax.ShapeDtypeStruct((64, 8, 1024), jnp.bfloat16),
            jax.ShapeDtypeStruct((2, 32, 1024), jnp.bfloat16),
        ],
        in_specs=[SMEM, VMEM],
        out_specs=[VMEM, VMEM],
        scratch_shapes=[
            pltpu.VMEM((2, TILES, ROWS + 8, LANES), jnp.float32),
            pltpu.VMEM((2, TILES, ROWS + 8, LANES), jnp.float32),
            pltpu.VMEM((WIDE, WIDE), jnp.bfloat16),
            pltpu.VMEM((WIDE, WIDE), jnp.bfloat16),
            pltpu.VMEM((2 * ROWS, 1024), jnp.bfloat16),
        ],
        compiler_params=params,
        cost_estimate=pl.CostEstimate(flops=60_000_000, bytes_accessed=2 << 20, transcendentals=3 << 20),
        name="inner",
    )(kappa, frames)
    whole = pl.pallas_call(
        edge_kernel,
        out_shape=jax.ShapeDtypeStruct((64, 8, 1024), jnp.bfloat16),
        in_specs=[SMEM, VMEM, VMEM, VMEM, ANY],
        out_specs=ANY,
        scratch_shapes=[
            pltpu.SemaphoreType.DMA((2,)),
            pltpu.VMEM((4, TILES, 24, LANES), jnp.float32),
            pltpu.VMEM((4, TILES, 24, LANES), jnp.float32),
            pltpu.VMEM((2, 8, 1024), jnp.bfloat16),
        ],
        input_output_aliases={4: 0},
        compiler_params=params,
        name="edges",
    )(kappa, ends, one, two, inner)
    return whole


def detrend(stored):
    block = pl.BlockSpec((64, 2, 4, CHUNK), lambda i: (0, 0, 0, i))
    shape = jax.ShapeDtypeStruct((64, 2, 4, 1024), jnp.bfloat16)
    return pl.pallas_call(
        detrend_kernel,
        grid=(1024 // CHUNK,),
        out_shape=[shape, shape],
        in_specs=[pl.BlockSpec((512, 256), lambda i: (0, 0)), pl.BlockSpec((64, 8, CHUNK), lambda i: (0, 0, i))],
        out_specs=[block, block],
        scratch_shapes=[pltpu.VMEM((64, 8, CHUNK), jnp.float32)],
        compiler_params=pltpu.CompilerParams(vmem_limit_bytes=24 * 1024 * 1024),
        name="detrend",
    )(band_weights(), stored)


def local(frames, kappa):
    blocks = diffuse(frames.reshape(2, ROWS, 1024), kappa)
    stored = lax.all_to_all(blocks, "vol", split_axis=0, concat_axis=0, tiled=True)
    dff, slope = detrend(stored)
    return dff.reshape(128, 1, 4, 1, 1024), slope.reshape(128, 1, 4, 1, 1024)


def solution(mesh):
    out = P(None, None, "vol", "strip", None)
    return jax.shard_map(
        local,
        mesh=mesh,
        in_specs=(P("vol", None, "strip", None), P("vol")),
        out_specs=(out, out),
        check_vma=False,
    )
```

```python
import functools
import math
import numpy as np
import jax
import jax.numpy as jnp
from jax import lax
from jax.experimental import pallas as pl
from jax.experimental.pallas import tpu as pltpu
from jax.sharding import PartitionSpec as P

PASSES = 3
BAND = 16
TIMES = 128
LANES = 128
TILES = 8
ROWS = 256
HALO = 4
GROUP = 4
WIDE = GROUP * LANES
MIX = 64
STARTS = (0, 64, 192, 256)
CHUNK = 512
ROOT5 = math.sqrt(5.0)


def band_weights():
    steps = np.arange(TIMES)
    gap = np.abs(steps[:, None] - steps[None, :])
    raw = np.where(gap <= BAND, BAND + 1 - gap, 0).astype(np.float32)
    weights = raw / np.sum(raw, axis=1, keepdims=True, dtype=np.float32)
    spread = np.kron(weights, np.eye(4, dtype=np.float32))
    blocks = [spread[128 * b : 128 * b + 128, k : k + 256] for b, k in enumerate(STARTS)]
    return jnp.asarray(np.concatenate(blocks, axis=0), jnp.bfloat16)


def flux(diff):
    return diff * pl.reciprocal(5.0 + diff * diff, approx=True)


def advance(pieces, below, above_flow, group):
    shape = pieces[0].shape
    lane = lax.broadcasted_iota(jnp.int32, shape, 1)
    last, first = lane == LANES - 1, lane == 0
    new = []
    before = flux(pieces[0])
    turned = pltpu.roll(pieces[0], LANES - 1, 1)
    for g in range(0, TILES, group):
        later = pltpu.roll(pieces[g + group], LANES - 1, 1) if g + group < TILES else jnp.zeros(shape, jnp.float32)
        right = list(pieces[g + 1 : g + group]) + [jnp.where(last, later, turned)]
        turned = later
        flow = [flux(right[t] - pieces[g + t]) for t in range(group)]
        moved = pltpu.roll(flow[-1], 1, 1)
        left = [jnp.where(first, before, moved)] + flow[:-1]
        before = moved
        for t in range(group):
            i = g + t
            down = flux(below[i] - pieces[i])
            up = above_flow(i, down)
            new.append(pieces[i] + ((down - up) + (flow[t] - left[t])))
    return new


def inner_kernel(kappa_ref, frames_ref, out_ref, ends_ref, field, flows, spread, gather, packed):
    source = lax.broadcasted_iota(jnp.int32, (WIDE, LANES), 0)
    lane = lax.broadcasted_iota(jnp.int32, (WIDE, LANES), 1)
    for t in range(GROUP):
        spread[:, t * LANES : (t + 1) * LANES] = (source == lane * GROUP + t).astype(jnp.float32).astype(jnp.bfloat16)
        place = (source & (LANES - 1)) * GROUP + lax.shift_right_logical(source, 7)
        gather[:, t * LANES : (t + 1) * LANES] = (place == lane + t * LANES).astype(jnp.float32).astype(jnp.bfloat16)
    units = [ROOT5 / jnp.full((8, LANES), kappa_ref[v], jnp.float32) for v in range(2)]
    backs = [jnp.full((8, LANES), kappa_ref[v], jnp.float32) * (1.0 / ROOT5) for v in range(2)]
    low = lax.broadcasted_iota(jnp.int32, (8, LANES), 0) < 4
    zero = jnp.zeros((8, LANES), jnp.float32)
    groups = TILES // GROUP
    for v in range(2):
        for i in range(TILES):
            field[v, i, ROWS : ROWS + 8, :] = zero
            flows[v, i, 0:8, :] = zero

    def fill(at):
        rows = [frames_ref[v, at : at + MIX, g * WIDE : (g + 1) * WIDE] for v in range(2) for g in range(groups)]
        value = jnp.dot(jnp.concatenate(rows, axis=0), spread[...], preferred_element_type=jnp.float32)
        for v in range(2):
            for i in range(TILES):
                g, t = i // GROUP, i % GROUP
                start = (v * groups + g) * MIX
                field[v, i, at : at + MIX, :] = value[start : start + MIX, t * LANES : (t + 1) * LANES] * units[v][0:1]

    def move(v, at):
        def above_flow(i, down):
            flows[v, i, pl.ds(at + 8, 8), :] = down
            return flows[v, i, pl.ds(at + 7, 8), :]

        pieces = [field[v, i, pl.ds(at, 8), :] for i in range(TILES)]
        below = [field[v, i, pl.ds(at + 1, 8), :] for i in range(TILES)]
        return advance(pieces, below, above_flow, GROUP)

    def empty(at):
        rows = [packed[at : at + 2 * MIX, g * WIDE : (g + 1) * WIDE] for g in range(groups)]
        value = jnp.dot(jnp.concatenate(rows, axis=0), gather[...], preferred_element_type=jnp.float32)
        value = value.astype(jnp.bfloat16)
        for g in range(groups):
            out_ref[at // 8 : (at + 2 * MIX) // 8, :, g * WIDE : (g + 1) * WIDE] = value[
                g * 2 * MIX : (g + 1) * 2 * MIX
            ].reshape(2 * MIX // 8, 8, WIDE)

    fill(0)
    for p in range(PASSES):
        for start in range(0, ROWS, MIX):
            if p == 0 and start + MIX < ROWS:
                fill(start + MIX)
            if p == PASSES - 1 and start:
                empty(2 * (start - MIX))
            for at in range(start, start + MIX, 8):
                new = [move(v, at) for v in range(2)]
                for i in range(TILES):
                    if p < PASSES - 1:
                        field[0, i, at : at + 8, :] = new[0][i]
                        field[1, i, at : at + 8, :] = new[1][i]
                    else:
                        a, b = new[0][i] * backs[0], new[1][i] * backs[1]
                        even = jnp.where(low, a, pltpu.roll(b, 4, 0))
                        odd = jnp.where(low, pltpu.roll(a, 4, 0), b)
                        both = jnp.concatenate([even, odd], axis=0).astype(jnp.bfloat16)
                        packed[2 * at : 2 * at + 16, i * LANES : (i + 1) * LANES] = both
    empty(2 * (ROWS - MIX))
    ends_ref[:, :16] = frames_ref[:, :16]
    ends_ref[:, 16:] = frames_ref[:, ROWS - 16 :]


def edge_kernel(kappa_ref, ends_ref, two_ref, one_ref, _, out_ref, sems, field, flows, blocks):
    strip = lax.axis_index("strip")
    even = lax.rem(strip, 2) == 0
    inside = (
        jnp.where(strip == 0, 0.0, 1.0).astype(jnp.float32),
        jnp.where(strip == lax.axis_size("strip") - 1, 0.0, 1.0).astype(jnp.float32),
    )
    low = lax.broadcasted_iota(jnp.int32, (8, LANES), 0) < 4
    zero = jnp.zeros((8, LANES), jnp.float32)
    spots = [slice(i * LANES, (i + 1) * LANES) for i in range(TILES)]
    for n in range(4):
        for i in range(TILES):
            field[n, i, 16:24, :] = zero
            flows[n, i, 0:8, :] = zero
    done = []
    for v in range(2):
        unit = ROOT5 / jnp.full((1, LANES), kappa_ref[v], jnp.float32)
        sides = []
        for side in range(2):
            if side == 0:
                own = ends_ref[v, :16].astype(jnp.float32)[0:8]
                far = jnp.where(even, two_ref[v].astype(jnp.float32), one_ref[v].astype(jnp.float32))
                window = [jnp.concatenate([far, far], axis=0), own]
            else:
                own = ends_ref[v, 16:].astype(jnp.float32)[8:16]
                far = jnp.where(even, one_ref[v].astype(jnp.float32), two_ref[v].astype(jnp.float32))
                window = [own, jnp.concatenate([far, far], axis=0)]
            mid = [[w[:, s] * unit for s in spots] for w in window]
            for p in range(PASSES):
                for k in range(2):
                    for i in range(TILES):
                        field[2 * v + side, i, 8 * k : 8 * k + 8, :] = mid[k][i]
                for k in range(2):
                    below = [field[2 * v + side, i, 8 * k + 1 : 8 * k + 9, :] for i in range(TILES)]

                    def above_flow(i, down, at=8 * k, n=2 * v + side):
                        flows[n, i, at + 8 : at + 16, :] = down
                        return flows[n, i, at + 7 : at + 15, :]

                    mid[k] = advance(mid[k], below, above_flow, 1)
                mid[side] = [value * inside[side] for value in mid[side]]
            sides.append([value * (kappa_ref[v] * (1.0 / ROOT5)) for value in mid[1 - side]])
        done.append(sides)
    for i in range(TILES):
        top = jnp.where(low, done[0][0][i], pltpu.roll(done[1][0][i], 4, 0))
        end = jnp.where(low, pltpu.roll(done[0][1][i], 4, 0), done[1][1][i])
        blocks[0, :, spots[i]] = top.astype(jnp.bfloat16)
        blocks[1, :, spots[i]] = end.astype(jnp.bfloat16)
    copies = [
        pltpu.make_async_copy(blocks.at[0], out_ref.at[0], sems.at[0]),
        pltpu.make_async_copy(blocks.at[1], out_ref.at[63], sems.at[1]),
    ]
    for copy in copies:
        copy.start()
    for copy in copies:
        copy.wait()


def detrend_kernel(weights_ref, stored_ref, dff_ref, slope_ref, ratio):
    stored = stored_ref[...].reshape(4 * TIMES, CHUNK)
    for b, k in enumerate(STARTS):
        baseline = jnp.dot(
            weights_ref[128 * b : 128 * b + 128, :], stored[k : k + 256], preferred_element_type=jnp.float32
        )
        value = stored[128 * b : 128 * b + 128].astype(jnp.float32)
        ratio[16 * b : 16 * b + 16] = ((value - baseline) / (baseline + 0.1)).reshape(16, 8, CHUNK)

    low = lax.broadcasted_iota(jnp.int32, (8, LANES), 0) < 4
    for i in range(CHUNK // LANES):
        spot = slice(i * LANES, (i + 1) * LANES)
        own = ratio[0, :, spot]
        turned = pltpu.roll(own, 4, 0)
        previous = None
        for j in range(TIMES // 2):
            if j + 1 < TIMES // 2:
                other = ratio[j + 1, :, spot]
                other_turned = pltpu.roll(other, 4, 0)
                between = jnp.where(low, turned, other_turned)
            else:
                other = other_turned = None
                between = turned
            if previous is None:
                slope = jnp.where(low, between - own, 0.5 * (between - turned))
            elif other is None:
                slope = jnp.where(low, 0.5 * (between - previous), own - previous)
            else:
                slope = 0.5 * (between - previous)
            dff_ref[j, 0, :, spot] = own[0:4].astype(jnp.bfloat16)
            dff_ref[j, 1, :, spot] = turned[0:4].astype(jnp.bfloat16)
            slope_ref[j, 0, :, spot] = slope[0:4].astype(jnp.bfloat16)
            slope_ref[j, 1, :, spot] = pltpu.roll(slope, 4, 0)[0:4].astype(jnp.bfloat16)
            own, turned, previous = other, other_turned, between


VMEM = pl.BlockSpec(memory_space=pltpu.VMEM)
SMEM = pl.BlockSpec(memory_space=pltpu.SMEM)
ANY = pl.BlockSpec(memory_space=pl.ANY)


def diffuse(frames, kappa):
    devices = lax.axis_size("strip")
    even = lax.rem(lax.axis_index("strip"), 2) == 0
    top, bottom = frames[:, :HALO], frames[:, ROWS - HALO :]
    first = [pair for i in range(0, devices - 1, 2) for pair in ((i, i + 1), (i + 1, i))]
    second = [pair for i in range(1, devices - 1, 2) for pair in ((i, i + 1), (i + 1, i))]
    two, one = lax.optimization_barrier((jnp.where(even, top, bottom), jnp.where(even, bottom, top)))
    two = lax.ppermute(two, "strip", second)
    one = lax.ppermute(one, "strip", first)
    params = pltpu.CompilerParams(vmem_limit_bytes=24 * 1024 * 1024)
    inner, ends = pl.pallas_call(
        inner_kernel,
        out_shape=[
            jax.ShapeDtypeStruct((64, 8, 1024), jnp.bfloat16),
            jax.ShapeDtypeStruct((2, 32, 1024), jnp.bfloat16),
        ],
        in_specs=[SMEM, VMEM],
        out_specs=[VMEM, VMEM],
        scratch_shapes=[
            pltpu.VMEM((2, TILES, ROWS + 8, LANES), jnp.float32),
            pltpu.VMEM((2, TILES, ROWS + 8, LANES), jnp.float32),
            pltpu.VMEM((WIDE, WIDE), jnp.bfloat16),
            pltpu.VMEM((WIDE, WIDE), jnp.bfloat16),
            pltpu.VMEM((2 * ROWS, 1024), jnp.bfloat16),
        ],
        compiler_params=params,
        cost_estimate=pl.CostEstimate(flops=60_000_000, bytes_accessed=2 << 20, transcendentals=3 << 20),
        name="inner",
    )(kappa, frames)
    whole = pl.pallas_call(
        edge_kernel,
        out_shape=jax.ShapeDtypeStruct((64, 8, 1024), jnp.bfloat16),
        in_specs=[SMEM, VMEM, VMEM, VMEM, ANY],
        out_specs=ANY,
        scratch_shapes=[
            pltpu.SemaphoreType.DMA((2,)),
            pltpu.VMEM((4, TILES, 24, LANES), jnp.float32),
            pltpu.VMEM((4, TILES, 24, LANES), jnp.float32),
            pltpu.VMEM((2, 8, 1024), jnp.bfloat16),
        ],
        input_output_aliases={4: 0},
        compiler_params=params,
        name="edges",
    )(kappa, ends, two, one, inner)
    return whole


def detrend(stored):
    block = pl.BlockSpec((64, 2, 4, CHUNK), lambda i: (0, 0, 0, i))
    shape = jax.ShapeDtypeStruct((64, 2, 4, 1024), jnp.bfloat16)
    return pl.pallas_call(
        detrend_kernel,
        grid=(1024 // CHUNK,),
        out_shape=[shape, shape],
        in_specs=[pl.BlockSpec((512, 256), lambda i: (0, 0)), pl.BlockSpec((64, 8, CHUNK), lambda i: (0, 0, i))],
        out_specs=[block, block],
        scratch_shapes=[pltpu.VMEM((64, 8, CHUNK), jnp.float32)],
        compiler_params=pltpu.CompilerParams(vmem_limit_bytes=24 * 1024 * 1024),
        name="detrend",
    )(band_weights(), stored)


def local(frames, kappa):
    blocks = diffuse(frames.reshape(2, ROWS, 1024), kappa)
    stored = lax.all_to_all(blocks, "vol", split_axis=0, concat_axis=0, tiled=True)
    dff, slope = detrend(stored)
    return dff.reshape(128, 1, 4, 1, 1024), slope.reshape(128, 1, 4, 1, 1024)


def solution(mesh):
    out = P(None, None, "vol", "strip", None)
    return jax.shard_map(
        local,
        mesh=mesh,
        in_specs=(P("vol", None, "strip", None), P("vol")),
        out_specs=(out, out),
        check_vma=False,
    )
```

```python
import functools
import math
import numpy as np
import jax
import jax.numpy as jnp
from jax import lax
from jax.experimental import pallas as pl
from jax.experimental.pallas import tpu as pltpu
from jax.sharding import PartitionSpec as P

PASSES = 3
BAND = 16
TIMES = 128
LANES = 128
TILES = 8
ROWS = 256
HALO = 4
GROUP = 4
WIDE = GROUP * LANES
MIX = 64
STARTS = (0, 64, 192, 256)
CHUNK = 512
ROOT5 = math.sqrt(5.0)


ROUNDS = ((0, 2, 5), (1, 3), (4, 6))


def is_upper(strip, uppers):
    found = strip == uppers[0]
    for i in uppers[1:]:
        found = found | (strip == i)
    return found


def band_weights():
    steps = np.arange(TIMES)
    gap = np.abs(steps[:, None] - steps[None, :])
    raw = np.where(gap <= BAND, BAND + 1 - gap, 0).astype(np.float32)
    weights = raw / np.sum(raw, axis=1, keepdims=True, dtype=np.float32)
    spread = np.kron(weights, np.eye(4, dtype=np.float32))
    blocks = [spread[128 * b : 128 * b + 128, k : k + 256] for b, k in enumerate(STARTS)]
    return jnp.asarray(np.concatenate(blocks, axis=0), jnp.bfloat16)


def flux(diff):
    return diff * pl.reciprocal(5.0 + diff * diff, approx=True)


def advance(pieces, below, above_flow, group):
    shape = pieces[0].shape
    lane = lax.broadcasted_iota(jnp.int32, shape, 1)
    last, first = lane == LANES - 1, lane == 0
    new = []
    before = flux(pieces[0])
    turned = pltpu.roll(pieces[0], LANES - 1, 1)
    for g in range(0, TILES, group):
        later = pltpu.roll(pieces[g + group], LANES - 1, 1) if g + group < TILES else jnp.zeros(shape, jnp.float32)
        right = list(pieces[g + 1 : g + group]) + [jnp.where(last, later, turned)]
        turned = later
        flow = [flux(right[t] - pieces[g + t]) for t in range(group)]
        moved = pltpu.roll(flow[-1], 1, 1)
        left = [jnp.where(first, before, moved)] + flow[:-1]
        before = moved
        for t in range(group):
            i = g + t
            down = flux(below[i] - pieces[i])
            up = above_flow(i, down)
            new.append(pieces[i] + ((down - up) + (flow[t] - left[t])))
    return new


def inner_kernel(kappa_ref, frames_ref, out_ref, ends_ref, field, flows, spread, gather, packed):
    source = lax.broadcasted_iota(jnp.int32, (WIDE, LANES), 0)
    lane = lax.broadcasted_iota(jnp.int32, (WIDE, LANES), 1)
    for t in range(GROUP):
        spread[:, t * LANES : (t + 1) * LANES] = (source == lane * GROUP + t).astype(jnp.float32).astype(jnp.bfloat16)
        place = (source & (LANES - 1)) * GROUP + lax.shift_right_logical(source, 7)
        gather[:, t * LANES : (t + 1) * LANES] = (place == lane + t * LANES).astype(jnp.float32).astype(jnp.bfloat16)
    units = [ROOT5 / jnp.full((8, LANES), kappa_ref[v], jnp.float32) for v in range(2)]
    backs = [jnp.full((8, LANES), kappa_ref[v], jnp.float32) * (1.0 / ROOT5) for v in range(2)]
    low = lax.broadcasted_iota(jnp.int32, (8, LANES), 0) < 4
    zero = jnp.zeros((8, LANES), jnp.float32)
    groups = TILES // GROUP
    for v in range(2):
        for i in range(TILES):
            field[v, i, ROWS : ROWS + 8, :] = zero
            flows[v, i, 0:8, :] = zero

    def fill(at):
        rows = [frames_ref[v, at : at + MIX, g * WIDE : (g + 1) * WIDE] for v in range(2) for g in range(groups)]
        value = jnp.dot(jnp.concatenate(rows, axis=0), spread[...], preferred_element_type=jnp.float32)
        for v in range(2):
            for i in range(TILES):
                g, t = i // GROUP, i % GROUP
                start = (v * groups + g) * MIX
                field[v, i, at : at + MIX, :] = value[start : start + MIX, t * LANES : (t + 1) * LANES] * units[v][0:1]

    def move(v, at):
        def above_flow(i, down):
            flows[v, i, pl.ds(at + 8, 8), :] = down
            return flows[v, i, pl.ds(at + 7, 8), :]

        pieces = [field[v, i, pl.ds(at, 8), :] for i in range(TILES)]
        below = [field[v, i, pl.ds(at + 1, 8), :] for i in range(TILES)]
        return advance(pieces, below, above_flow, GROUP)

    def empty(at):
        rows = [packed[at : at + 2 * MIX, g * WIDE : (g + 1) * WIDE] for g in range(groups)]
        value = jnp.dot(jnp.concatenate(rows, axis=0), gather[...], preferred_element_type=jnp.float32)
        value = value.astype(jnp.bfloat16)
        for g in range(groups):
            out_ref[at // 8 : (at + 2 * MIX) // 8, :, g * WIDE : (g + 1) * WIDE] = value[
                g * 2 * MIX : (g + 1) * 2 * MIX
            ].reshape(2 * MIX // 8, 8, WIDE)

    fill(0)
    for p in range(PASSES):
        for start in range(0, ROWS, MIX):
            if p == 0 and start + MIX < ROWS:
                fill(start + MIX)
            if p == PASSES - 1 and start:
                empty(2 * (start - MIX))
            for at in range(start, start + MIX, 8):
                new = [move(v, at) for v in range(2)]
                for i in range(TILES):
                    if p < PASSES - 1:
                        field[0, i, at : at + 8, :] = new[0][i]
                        field[1, i, at : at + 8, :] = new[1][i]
                    else:
                        a, b = new[0][i] * backs[0], new[1][i] * backs[1]
                        even = jnp.where(low, a, pltpu.roll(b, 4, 0))
                        odd = jnp.where(low, pltpu.roll(a, 4, 0), b)
                        both = jnp.concatenate([even, odd], axis=0).astype(jnp.bfloat16)
                        packed[2 * at : 2 * at + 16, i * LANES : (i + 1) * LANES] = both
    empty(2 * (ROWS - MIX))
    ends_ref[:, :16] = frames_ref[:, :16]
    ends_ref[:, 16:] = frames_ref[:, ROWS - 16 :]


def edge_kernel(kappa_ref, ends_ref, one_ref, two_ref, three_ref, _, out_ref, sems, field, flows, blocks):
    strip = lax.axis_index("strip")
    got = [(is_upper(strip, r), ref) for r, ref in zip(ROUNDS, (one_ref, two_ref, three_ref))]
    inside = (
        jnp.where(strip == 0, 0.0, 1.0).astype(jnp.float32),
        jnp.where(strip == lax.axis_size("strip") - 1, 0.0, 1.0).astype(jnp.float32),
    )
    low = lax.broadcasted_iota(jnp.int32, (8, LANES), 0) < 4
    zero = jnp.zeros((8, LANES), jnp.float32)
    spots = [slice(i * LANES, (i + 1) * LANES) for i in range(TILES)]
    for n in range(4):
        for i in range(TILES):
            field[n, i, 16:24, :] = zero
            flows[n, i, 0:8, :] = zero
    done = []
    for v in range(2):
        unit = ROOT5 / jnp.full((1, LANES), kappa_ref[v], jnp.float32)
        sides = []
        for side in range(2):
            if side == 0:
                own = ends_ref[v, :16].astype(jnp.float32)[0:8]
                far = sum(jnp.where(upper, 0.0, ref[v].astype(jnp.float32)) for upper, ref in got)
                window = [jnp.concatenate([far, far], axis=0), own]
            else:
                own = ends_ref[v, 16:].astype(jnp.float32)[8:16]
                far = sum(jnp.where(upper, ref[v].astype(jnp.float32), 0.0) for upper, ref in got)
                window = [own, jnp.concatenate([far, far], axis=0)]
            mid = [[w[:, s] * unit for s in spots] for w in window]
            for p in range(PASSES):
                for k in range(2):
                    for i in range(TILES):
                        field[2 * v + side, i, 8 * k : 8 * k + 8, :] = mid[k][i]
                for k in range(2):
                    below = [field[2 * v + side, i, 8 * k + 1 : 8 * k + 9, :] for i in range(TILES)]

                    def above_flow(i, down, at=8 * k, n=2 * v + side):
                        flows[n, i, at + 8 : at + 16, :] = down
                        return flows[n, i, at + 7 : at + 15, :]

                    mid[k] = advance(mid[k], below, above_flow, 1)
                mid[side] = [value * inside[side] for value in mid[side]]
            sides.append([value * (kappa_ref[v] * (1.0 / ROOT5)) for value in mid[1 - side]])
        done.append(sides)
    for i in range(TILES):
        top = jnp.where(low, done[0][0][i], pltpu.roll(done[1][0][i], 4, 0))
        end = jnp.where(low, pltpu.roll(done[0][1][i], 4, 0), done[1][1][i])
        blocks[0, :, spots[i]] = top.astype(jnp.bfloat16)
        blocks[1, :, spots[i]] = end.astype(jnp.bfloat16)
    copies = [
        pltpu.make_async_copy(blocks.at[0], out_ref.at[0], sems.at[0]),
        pltpu.make_async_copy(blocks.at[1], out_ref.at[63], sems.at[1]),
    ]
    for copy in copies:
        copy.start()
    for copy in copies:
        copy.wait()


def detrend_kernel(weights_ref, stored_ref, dff_ref, slope_ref, ratio):
    stored = stored_ref[...].reshape(4 * TIMES, CHUNK)
    for b, k in enumerate(STARTS):
        baseline = jnp.dot(
            weights_ref[128 * b : 128 * b + 128, :], stored[k : k + 256], preferred_element_type=jnp.float32
        )
        value = stored[128 * b : 128 * b + 128].astype(jnp.float32)
        ratio[16 * b : 16 * b + 16] = ((value - baseline) / (baseline + 0.1)).reshape(16, 8, CHUNK)

    low = lax.broadcasted_iota(jnp.int32, (8, LANES), 0) < 4
    for i in range(CHUNK // LANES):
        spot = slice(i * LANES, (i + 1) * LANES)
        own = ratio[0, :, spot]
        turned = pltpu.roll(own, 4, 0)
        previous = None
        for j in range(TIMES // 2):
            if j + 1 < TIMES // 2:
                other = ratio[j + 1, :, spot]
                other_turned = pltpu.roll(other, 4, 0)
                between = jnp.where(low, turned, other_turned)
            else:
                other = other_turned = None
                between = turned
            if previous is None:
                slope = jnp.where(low, between - own, 0.5 * (between - turned))
            elif other is None:
                slope = jnp.where(low, 0.5 * (between - previous), own - previous)
            else:
                slope = 0.5 * (between - previous)
            dff_ref[j, 0, :, spot] = own[0:4].astype(jnp.bfloat16)
            dff_ref[j, 1, :, spot] = turned[0:4].astype(jnp.bfloat16)
            slope_ref[j, 0, :, spot] = slope[0:4].astype(jnp.bfloat16)
            slope_ref[j, 1, :, spot] = pltpu.roll(slope, 4, 0)[0:4].astype(jnp.bfloat16)
            own, turned, previous = other, other_turned, between


VMEM = pl.BlockSpec(memory_space=pltpu.VMEM)
SMEM = pl.BlockSpec(memory_space=pltpu.SMEM)
ANY = pl.BlockSpec(memory_space=pl.ANY)


def diffuse(frames, kappa):
    top, bottom = frames[:, :HALO], frames[:, ROWS - HALO :]
    strip = lax.axis_index("strip")
    sent = lax.optimization_barrier(tuple(jnp.where(is_upper(strip, r), bottom, top) for r in ROUNDS))
    swaps = [[pair for i in r for pair in ((i, i + 1), (i + 1, i))] for r in ROUNDS]
    got = [lax.ppermute(rows, "strip", swap) for rows, swap in zip(sent, swaps)]
    params = pltpu.CompilerParams(vmem_limit_bytes=24 * 1024 * 1024)
    inner, ends = pl.pallas_call(
        inner_kernel,
        out_shape=[
            jax.ShapeDtypeStruct((64, 8, 1024), jnp.bfloat16),
            jax.ShapeDtypeStruct((2, 32, 1024), jnp.bfloat16),
        ],
        in_specs=[SMEM, VMEM],
        out_specs=[VMEM, VMEM],
        scratch_shapes=[
            pltpu.VMEM((2, TILES, ROWS + 8, LANES), jnp.float32),
            pltpu.VMEM((2, TILES, ROWS + 8, LANES), jnp.float32),
            pltpu.VMEM((WIDE, WIDE), jnp.bfloat16),
            pltpu.VMEM((WIDE, WIDE), jnp.bfloat16),
            pltpu.VMEM((2 * ROWS, 1024), jnp.bfloat16),
        ],
        compiler_params=params,
        cost_estimate=pl.CostEstimate(flops=60_000_000, bytes_accessed=2 << 20, transcendentals=3 << 20),
        name="inner",
    )(kappa, frames)
    whole = pl.pallas_call(
        edge_kernel,
        out_shape=jax.ShapeDtypeStruct((64, 8, 1024), jnp.bfloat16),
        in_specs=[SMEM, VMEM, VMEM, VMEM, VMEM, ANY],
        out_specs=ANY,
        scratch_shapes=[
            pltpu.SemaphoreType.DMA((2,)),
            pltpu.VMEM((4, TILES, 24, LANES), jnp.float32),
            pltpu.VMEM((4, TILES, 24, LANES), jnp.float32),
            pltpu.VMEM((2, 8, 1024), jnp.bfloat16),
        ],
        input_output_aliases={5: 0},
        compiler_params=params,
        name="edges",
    )(kappa, ends, *got, inner)
    return whole


def detrend(stored):
    block = pl.BlockSpec((64, 2, 4, CHUNK), lambda i: (0, 0, 0, i))
    shape = jax.ShapeDtypeStruct((64, 2, 4, 1024), jnp.bfloat16)
    return pl.pallas_call(
        detrend_kernel,
        grid=(1024 // CHUNK,),
        out_shape=[shape, shape],
        in_specs=[pl.BlockSpec((512, 256), lambda i: (0, 0)), pl.BlockSpec((64, 8, CHUNK), lambda i: (0, 0, i))],
        out_specs=[block, block],
        scratch_shapes=[pltpu.VMEM((64, 8, CHUNK), jnp.float32)],
        compiler_params=pltpu.CompilerParams(vmem_limit_bytes=24 * 1024 * 1024),
        name="detrend",
    )(band_weights(), stored)


def local(frames, kappa):
    blocks = diffuse(frames.reshape(2, ROWS, 1024), kappa)
    stored = lax.all_to_all(blocks, "vol", split_axis=0, concat_axis=0, tiled=True)
    dff, slope = detrend(stored)
    return dff.reshape(128, 1, 4, 1, 1024), slope.reshape(128, 1, 4, 1, 1024)


def solution(mesh):
    out = P(None, None, "vol", "strip", None)
    return jax.shard_map(
        local,
        mesh=mesh,
        in_specs=(P("vol", None, "strip", None), P("vol")),
        out_specs=(out, out),
        check_vma=False,
    )
```
